32 devices in a mesh: groups: 2 (over x), row: 16 (over z, y, core).
Axes of the slice: x: 2, y: 2, z: 4, core: 2. Of those that a mesh axis runs over, the one named last changes fastest.
Arguments:
- forces: bfloat16 [2048, 768], P(('groups', 'row')), parts along dimension 0, may hold values from -6 to 6
- tiles: bfloat16 [32768, 96, 96], P(('groups', 'row')), parts along dimension 0, may hold values from -0.109375 to 0.109375
- tile_local: int32 [32768], P(('groups', 'row')), parts along dimension 0, may hold values from 0 to 63
- tile_slot: int32 [32768], P(('groups', 'row')), parts along dimension 0, may hold values from 0 to 255
- tile_flag: int32 [32768], P(('groups', 'row')), parts along dimension 0, may hold values 0 or 1
- want_list: int32 [32, 16, 16], P(('groups', 'row')), parts along dimension 0, may hold values from 0 to 63
Outputs:
- krylov_one: bfloat16 [2048, 768], P(('groups', 'row')), parts along dimension 0
- krylov_two: bfloat16 [2048, 768], P(('groups', 'row')), parts along dimension 0
The draws below stay inside these ranges and needn't reach their ends.
There are 2 independent parts, one for each index of `groups`. The reference program is written for one: setup_inputs(seed, part) draws one part's arguments, and reference() takes and returns one part's arrays. A program takes and returns all parts, laid end to end along the dimension named above; each array names one. Nothing has to cross between parts.
All inputs are finite; a program needn't handle non-finite values. No bound on the sum of `tile_flag` on one device may be relied on, other than what follows from the above.
Results may differ from the reference program's by a relative error of at most 0.0041.
Values may be sent and summed in bfloat16 or wider, within the bound.
A program may use at most 128 MiB of HBM per device.

```python
import jax
import jax.numpy as jnp
from jax import lax

UNK = 96
NRHS = 8
WIDTH = 768
FD = 64
TILE_DEV = 1024
CAP = 16
BLOCKS = 16
FIBRES = 1024
TILES = 16384
SLOTS = 256
N_ROW = 16


def set_ends(result, rng, low, high):
    index_at = [jax.random.randint(jax.random.fold_in(rng, axis), (), 0, length) for axis, length in enumerate(result.shape)]
    longest = result.shape.index(max(result.shape))
    next_to = index_at[:longest] + [(index_at[longest] + 1) % result.shape[longest]] + index_at[longest + 1:]
    return result.at[tuple(index_at)].set(low).at[tuple(next_to)].set(high)


def shard_levels(stream_key, shape, cuts, least, top_value):
    def one(dim, blocks):
        draws = jax.random.uniform(jax.random.fold_in(jax.random.fold_in(stream_key, 6), dim), (blocks,), jnp.float32, least / len(cuts), top_value / len(cuts))
        return jnp.repeat(jnp.exp(draws), shape[dim] // blocks).reshape((-1,) + (1,) * (len(shape) - dim - 1))

    level = one(*cuts[0])
    for cut in cuts[1:]:
        level = level * one(*cut)
    return level


def noise(rng, shape, spread, reach, split=(), kind=jnp.bfloat16):
    array = spread * jax.random.normal(rng, shape, jnp.float32)
    if split:
        array = array * shard_levels(rng, shape, split, -0.22, 0.18)
    return jnp.clip(array, -reach, reach).astype(kind)


def setup_inputs(seed: int = 0, part: int = 0) -> dict:
    splits = jax.random.split(jax.random.key(seed), 7)
    own_keys = jax.random.split(jax.random.fold_in(splits[6], part), 7)
    forces = noise(own_keys[0], (FIBRES, WIDTH), 1.0, 6.0, ((0, 16),))
    tiles = noise(own_keys[1], (TILES, UNK, UNK), (UNK * 2 * TILE_DEV // FD) ** -0.5, 0.109375, ((0, 16),))
    tile_local = set_ends(jax.random.randint(own_keys[2], (TILES,), 0, FD), jax.random.fold_in(own_keys[2], 1), 0, FD - 1).astype(jnp.int32)
    tile_slot = set_ends(jax.random.randint(own_keys[3], (TILES,), 0, SLOTS), jax.random.fold_in(own_keys[3], 1), 0, SLOTS - 1).astype(jnp.int32)
    tile_flag = set_ends((jax.random.randint(own_keys[4], (TILES,), 0, 4) < 3).astype(jnp.int32), jax.random.fold_in(own_keys[4], 1), 0, 1)
    want_list = set_ends(jax.random.randint(own_keys[5], (BLOCKS, BLOCKS, CAP), 0, FD), jax.random.fold_in(own_keys[5], 1), 0, FD - 1).astype(jnp.int32)
    return {"forces": forces, "tiles": tiles, "tile_local": tile_local, "tile_slot": tile_slot, "tile_flag": tile_flag, "want_list": want_list}


def apply_mobility(field, tiles, tile_local, tile_slot, tile_flag, want_list):
    tile_blocks = tiles.reshape(N_ROW, TILE_DEV, UNK, UNK)
    local_blocks = tile_local.reshape(N_ROW, TILE_DEV)
    slot_blocks = tile_slot.reshape(N_ROW, TILE_DEV)
    flag_blocks = tile_flag.reshape(N_ROW, TILE_DEV)
    block_ids = jnp.arange(N_ROW, dtype=jnp.int32)

    def step(total, inputs):
        blocks, local, slot, flag, wanted, block_id = inputs
        peer = (slot // CAP).astype(jnp.int32)
        column = (slot % CAP).astype(jnp.int32)
        far_rows = (peer * FD + wanted[peer, column]).astype(jnp.int32)
        near_rows = (block_id * FD + local).astype(jnp.int32)
        far_vals = field[far_rows].astype(jnp.float32).reshape(TILE_DEV, NRHS, UNK)
        near_vals = field[near_rows].astype(jnp.float32).reshape(TILE_DEV, NRHS, UNK)
        tiles_wide = blocks.astype(jnp.float32)
        direct = jnp.einsum("kij,krj->kri", tiles_wide, far_vals, precision=lax.Precision.HIGHEST)
        mirror = jnp.einsum("kij,kri->krj", tiles_wide, near_vals, precision=lax.Precision.HIGHEST)
        mirror = mirror * flag.astype(jnp.float32)[:, None, None]
        total = total.at[near_rows].add(direct.reshape(TILE_DEV, WIDTH))
        total = total.at[far_rows].add(mirror.reshape(TILE_DEV, WIDTH))
        return total, None

    start = jnp.zeros((FIBRES, WIDTH), jnp.float32)
    total, unused = lax.scan(step, start, (tile_blocks, local_blocks, slot_blocks, flag_blocks, want_list, block_ids))
    return total


def reference(forces, tiles, tile_local, tile_slot, tile_flag, want_list):
    krylov_one = apply_mobility(forces, tiles, tile_local, tile_slot, tile_flag, want_list).astype(jnp.bfloat16)
    krylov_two = apply_mobility(krylov_one, tiles, tile_local, tile_slot, tile_flag, want_list).astype(jnp.bfloat16)
    return (krylov_one, krylov_two)
```

```python
import functools

import jax
import jax.numpy as jnp
from jax import lax
from jax.experimental import pallas as pl
from jax.experimental.pallas import tpu as pltpu
from jax.sharding import PartitionSpec as P

NRHS = 8
BANKS = 4
UNROLL = 16
BLOCK = 128


def pass_kernel(mirrored, pick_s, put_s, flag_s, tiles_ref, table_ref, out_ref, acc_ref):
    step = pl.program_id(0)

    @pl.when(step == 0)
    def _():
        acc_ref[...] = jnp.zeros_like(acc_ref)

    base = step * BLOCK

    def group(g, carry):
        start = pl.multiple_of(g * UNROLL, UNROLL)
        products = []
        for u in range(UNROLL):
            k = base + start + u
            x = table_ref[pick_s[k]]
            tile = tiles_ref[start + u]
            if mirrored:
                x = (x.astype(jnp.float32) * flag_s[k].astype(jnp.float32)).astype(jnp.bfloat16)
                dims = (((1,), (0,)), ((), ()))
            else:
                dims = (((1,), (1,)), ((), ()))
            products.append(lax.dot_general(x, tile, dims, preferred_element_type=jnp.float32))
        for u in range(UNROLL):
            row = put_s[base + start + u]
            acc_ref[u % BANKS, row] += products[u]
        return carry

    lax.fori_loop(0, BLOCK // UNROLL, group, 0)

    @pl.when(step == pl.num_programs(0) - 1)
    def _():
        out_ref[...] = (acc_ref[0] + acc_ref[1]) + (acc_ref[2] + acc_ref[3])


def tile_pass(mirrored, pick, put, flag, tiles, table, rows):
    count, unknowns = tiles.shape[0], tiles.shape[1]
    return pl.pallas_call(
        functools.partial(pass_kernel, mirrored),
        out_shape=jax.ShapeDtypeStruct((rows, NRHS, unknowns), jnp.float32),
        grid_spec=pltpu.PrefetchScalarGridSpec(
            num_scalar_prefetch=3,
            grid=(count // BLOCK,),
            in_specs=[
                pl.BlockSpec((BLOCK, unknowns, unknowns), lambda s, *_: (s, 0, 0)),
                pl.BlockSpec(table.shape, lambda s, *_: (0, 0, 0)),
            ],
            out_specs=pl.BlockSpec((rows, NRHS, unknowns), lambda s, *_: (0, 0, 0)),
            scratch_shapes=[pltpu.VMEM((BANKS, rows, NRHS, unknowns), jnp.float32)],
        ),
        compiler_params=pltpu.CompilerParams(vmem_limit_bytes=48 * 2**20),
        cost_estimate=pl.CostEstimate(
            flops=2 * count * NRHS * unknowns * unknowns,
            bytes_accessed=2 * count * unknowns * 128,
            transcendentals=0,
        ),
        name="mirror_pass" if mirrored else "direct_pass",
    )(pick, put, flag, tiles, table)


def combine_kernel(row_s, own_ref, got_ref, out_ref, acc_ref):
    acc_ref[0] = own_ref[...]
    for b in range(1, BANKS):
        acc_ref[b] = jnp.zeros(acc_ref.shape[1:], acc_ref.dtype)

    def group(g, carry):
        start = pl.multiple_of(g * UNROLL, UNROLL)
        for u in range(UNROLL):
            acc_ref[u % BANKS, row_s[start + u]] += got_ref[start + u]
        return carry

    lax.fori_loop(0, got_ref.shape[0] // UNROLL, group, 0)
    total = (acc_ref[0] + acc_ref[1]) + (acc_ref[2] + acc_ref[3])
    out_ref[...] = total.astype(out_ref.dtype)


def combine(rows, own, got):
    vmem = pl.BlockSpec(memory_space=pltpu.VMEM)
    return pl.pallas_call(
        combine_kernel,
        out_shape=jax.ShapeDtypeStruct(own.shape, jnp.bfloat16),
        in_specs=[pl.BlockSpec(memory_space=pltpu.SMEM), vmem, vmem],
        out_specs=vmem,
        scratch_shapes=[pltpu.VMEM((BANKS,) + own.shape, jnp.float32)],
        compiler_params=pltpu.CompilerParams(vmem_limit_bytes=32 * 2**20),
        name="combine_rows",
    )(rows, own, got)


def per_device(forces, tiles, tile_local, tile_slot, tile_flag, want_list):
    peers = lax.axis_size("row")
    fibres, width = forces.shape
    unknowns = tiles.shape[1]
    capacity = want_list.shape[2]
    slots = peers * capacity
    wanted = want_list[0]
    asked = lax.all_to_all(wanted, "row", 0, 0, tiled=True).reshape(-1)
    far_table = (jnp.arange(peers, dtype=jnp.int32)[:, None] * fibres + wanted).reshape(-1)
    slot_hot = tile_slot[:, None] == jnp.arange(slots, dtype=jnp.int32)[None, :]
    far_row = jnp.sum(jnp.where(slot_hot, far_table[None, :], 0), axis=1)

    def operate(current):
        everyone = lax.all_gather(current, "row", axis=0, tiled=True)
        slot_part = tile_pass(True, tile_local, tile_slot, tile_flag, tiles, current, slots)
        got = lax.all_to_all(slot_part, "row", 0, 0, tiled=True)
        own_part = tile_pass(False, far_row, tile_local, tile_flag, tiles, everyone, fibres)
        return combine(asked, own_part, got)

    one = operate(forces.reshape(fibres, NRHS, unknowns))
    two = operate(one)
    return (one.reshape(fibres, width), two.reshape(fibres, width))


def solution(mesh):
    in_specs = (
        P(("groups", "row"), None),
        P(("groups", "row"), None, None),
        P(("groups", "row")),
        P(("groups", "row")),
        P(("groups", "row")),
        P(("groups", "row"), None, None),
    )
    out_specs = (P(("groups", "row"), None), P(("groups", "row"), None))
    return jax.shard_map(
        per_device, mesh=mesh, in_specs=in_specs, out_specs=out_specs, check_vma=False
    )
```

```python
import functools

import jax
import jax.numpy as jnp
from jax import lax
from jax.experimental import pallas as pl
from jax.experimental.pallas import tpu as pltpu
from jax.sharding import PartitionSpec as P

NRHS = 8
BANKS = 4
UNROLL = 64
ROWS = 16
BLOCK = 128


def pass_kernel(mirrored, pick_s, put_s, flag_s, tiles_ref, table_ref, out_ref, near_ref, *banks):
    step = pl.program_id(0)
    unknowns = tiles_ref.shape[1]
    pair = BANKS // 2

    @pl.when(step == 0)
    def _():
        for bank in banks:
            bank[...] = jnp.zeros_like(bank)
        values = table_ref[...].astype(jnp.float32)
        if mirrored:
            blank = jnp.zeros_like(values)
            near_ref[0] = jnp.concatenate([values, blank], axis=2)
            near_ref[1] = jnp.concatenate([blank, values], axis=2)
        else:
            near_ref[0] = values

    base = step * BLOCK

    def operand(k, side):
        if mirrored:
            return near_ref[side, pick_s[k]] * flag_s[k].astype(jnp.float32)
        return near_ref[0, pick_s[k]]

    def group(g, carry):
        start = pl.multiple_of(g * UNROLL, UNROLL)
        for u in range(0, UNROLL, 2):
            k = base + start + u
            both = jnp.concatenate([operand(k, 0), operand(k + 1, 1)], axis=0).astype(jnp.bfloat16)
            stacked = tiles_ref[pl.ds(start + u, 2)].reshape(2 * unknowns, unknowns)
            dims = (((1,), (0 if mirrored else 1,)), ((), ()))
            product = lax.dot_general(both, stacked, dims, preferred_element_type=jnp.float32)
            which = (u // 2) % pair
            banks[2 * which][put_s[k]] += product[:NRHS, :unknowns]
            banks[2 * which + 1][put_s[k + 1]] += product[NRHS:]
        return carry

    lax.fori_loop(0, BLOCK // UNROLL, group, 0)

    @pl.when(step == pl.num_programs(0) - 1)
    def _():
        even, odd = banks[0][...], banks[1][...]
        for which in range(1, pair):
            even += banks[2 * which][...]
            odd += banks[2 * which + 1][...]
        out_ref[...] = even + odd[:, :, odd.shape[2] - unknowns:]


def tile_pass(mirrored, pick, put, flag, tiles, table, rows):
    count, unknowns = tiles.shape[0], tiles.shape[1]
    near = pltpu.VMEM(
        (2, table.shape[0], NRHS, 2 * unknowns) if mirrored else (1,) + table.shape, jnp.float32
    )
    return pl.pallas_call(
        functools.partial(pass_kernel, mirrored),
        out_shape=jax.ShapeDtypeStruct((rows, NRHS, unknowns), jnp.float32),
        grid_spec=pltpu.PrefetchScalarGridSpec(
            num_scalar_prefetch=3,
            grid=(count // BLOCK,),
            in_specs=[
                pl.BlockSpec((BLOCK, unknowns, unknowns), lambda s, *_: (s, 0, 0)),
                pl.BlockSpec(table.shape, lambda s, *_: (0, 0, 0)),
            ],
            out_specs=pl.BlockSpec((rows, NRHS, unknowns), lambda s, *_: (0, 0, 0)),
            scratch_shapes=[near]
            + [
                pltpu.VMEM((rows, NRHS, unknowns * (1 if mirrored or b % 2 == 0 else 2)), jnp.float32)
                for b in range(BANKS)
            ],
        ),
        compiler_params=pltpu.CompilerParams(vmem_limit_bytes=48 * 2**20),
        cost_estimate=pl.CostEstimate(
            flops=2 * count * NRHS * unknowns * unknowns,
            bytes_accessed=2 * count * unknowns * 128,
            transcendentals=0,
        ),
        name="mirror_pass" if mirrored else "direct_pass",
    )(pick, put, flag, tiles, table)


def gather_kernel(row_s, from_ref, out_ref, wide_ref):
    wide_ref[...] = from_ref[...].astype(jnp.float32)
    send_rows(row_s, wide_ref, out_ref)


def send_rows(row_s, wide_ref, out_ref):
    def group(g, carry):
        start = pl.multiple_of(g * ROWS, ROWS)
        for u in range(ROWS):
            out_ref[start + u] = wide_ref[row_s[start + u]].astype(out_ref.dtype)
        return carry

    lax.fori_loop(0, out_ref.shape[0] // ROWS, group, 0)


def gather(rows, table):
    vmem = pl.BlockSpec(memory_space=pltpu.VMEM)
    return pl.pallas_call(
        gather_kernel,
        out_shape=jax.ShapeDtypeStruct(rows.shape + table.shape[1:], jnp.bfloat16),
        in_specs=[pl.BlockSpec(memory_space=pltpu.SMEM), vmem],
        out_specs=vmem,
        scratch_shapes=[pltpu.VMEM(table.shape, jnp.float32)],
        compiler_params=pltpu.CompilerParams(vmem_limit_bytes=32 * 2**20),
        name="gather_rows",
    )(rows, table)


def combine_kernel(row_s, own_ref, got_ref, out_ref, *rest):
    banks = rest[-BANKS:]
    banks[0][...] = own_ref[...]
    for bank in banks[1:]:
        bank[...] = jnp.zeros_like(bank)

    def group(g, carry):
        start = pl.multiple_of(g * ROWS, ROWS)
        for u in range(ROWS):
            banks[u % BANKS][row_s[start + u]] += got_ref[start + u]
        return carry

    lax.fori_loop(0, got_ref.shape[0] // ROWS, group, 0)
    total = banks[0][...]
    for bank in banks[1:]:
        total += bank[...]
    out_ref[...] = total.astype(out_ref.dtype)
    if len(rest) > BANKS:
        banks[0][...] = total
        send_rows(row_s, banks[0], rest[0])


def combine(rows, own, got, send):
    vmem = pl.BlockSpec(memory_space=pltpu.VMEM)
    out = [jax.ShapeDtypeStruct(own.shape, jnp.bfloat16)]
    if send:
        out.append(jax.ShapeDtypeStruct(got.shape, jnp.bfloat16))
    return pl.pallas_call(
        combine_kernel,
        out_shape=out,
        in_specs=[pl.BlockSpec(memory_space=pltpu.SMEM), vmem, vmem],
        out_specs=[vmem] * len(out),
        scratch_shapes=[pltpu.VMEM(own.shape, jnp.float32)] * BANKS,
        compiler_params=pltpu.CompilerParams(vmem_limit_bytes=32 * 2**20),
        name="combine_rows",
    )(rows, own, got)


def per_device(forces, tiles, tile_local, tile_slot, tile_flag, want_list):
    peers = lax.axis_size("row")
    fibres, width = forces.shape
    unknowns = tiles.shape[1]
    capacity = want_list.shape[2]
    slots = peers * capacity
    wanted = want_list[0]
    asked = lax.all_to_all(wanted, "row", 0, 0, tiled=True).reshape(-1)
    def operate(current, sent, again):
        far = lax.all_to_all(sent, "row", 0, 0, tiled=True)
        slot_part = tile_pass(True, tile_local, tile_slot, tile_flag, tiles, current, slots)
        got = lax.all_to_all(slot_part, "row", 0, 0, tiled=True)
        own_part = tile_pass(False, tile_slot, tile_local, tile_flag, tiles, far, fibres)
        return combine(asked, own_part, got, again)

    start = forces.reshape(fibres, NRHS, unknowns)
    one, sent = operate(start, gather(asked, start), True)
    (two,) = operate(one, sent, False)
    return (one.reshape(fibres, width), two.reshape(fibres, width))


def solution(mesh):
    in_specs = (
        P(("groups", "row"), None),
        P(("groups", "row"), None, None),
        P(("groups", "row")),
        P(("groups", "row")),
        P(("groups", "row")),
        P(("groups", "row"), None, None),
    )
    out_specs = (P(("groups", "row"), None), P(("groups", "row"), None))
    return jax.shard_map(
        per_device, mesh=mesh, in_specs=in_specs, out_specs=out_specs, check_vma=False
    )
```

```python
import functools

import jax
import jax.numpy as jnp
from jax import lax
from jax.experimental import pallas as pl
from jax.experimental.pallas import tpu as pltpu
from jax.sharding import PartitionSpec as P

NRHS = 8
BANKS = 4
UNROLL = 64
LANES = 128
ROWS = 16
BLOCK = 128


def pair_kernel(tiles_ref, out_ref, turned_ref):
    unknowns = tiles_ref.shape[0]
    half = BLOCK // 2
    blank = jnp.zeros((LANES - unknowns, BLOCK), tiles_ref.dtype)

    def turn(g, carry):
        for u in range(8):
            i = g * 8 + u
            turned = jnp.concatenate([tiles_ref[i], blank], axis=0).T
            turned_ref[pl.ds(pl.multiple_of(i * BLOCK, BLOCK), BLOCK), :] = turned.astype(jnp.float32)
        return carry

    lax.fori_loop(0, unknowns // 8, turn, 0)

    def place(g, carry):
        for u in range(4):
            p = g * 4 + u
            low = turned_ref[pl.ds(p, unknowns, stride=BLOCK), :]
            high = turned_ref[pl.ds(p + half, unknowns, stride=BLOCK), :]
            out_ref[p] = jnp.concatenate([low, high], axis=1).astype(out_ref.dtype)
        return carry

    lax.fori_loop(0, half // 4, place, 0)


def pair_tiles(tiles):
    count, unknowns = tiles.shape[0], tiles.shape[1]
    return pl.pallas_call(
        pair_kernel,
        out_shape=jax.ShapeDtypeStruct((count // 2, unknowns, 2 * LANES), tiles.dtype),
        grid=(count // BLOCK,),
        in_specs=[pl.BlockSpec((unknowns, unknowns, BLOCK), lambda s: (0, 0, s))],
        out_specs=pl.BlockSpec((BLOCK // 2, unknowns, 2 * LANES), lambda s: (s, 0, 0)),
        scratch_shapes=[pltpu.VMEM((unknowns * BLOCK, LANES), jnp.float32)],
        compiler_params=pltpu.CompilerParams(vmem_limit_bytes=48 * 2**20),
        cost_estimate=pl.CostEstimate(flops=0, bytes_accessed=44 * 2**20, transcendentals=0),
        name="pair_tiles",
    )(jnp.transpose(tiles, (1, 2, 0)))


def pass_kernel(mirrored, pick_s, put_s, flag_s, pairs_ref, table_ref, out_ref, near_ref, *banks):
    step = pl.program_id(0)
    unknowns = pairs_ref.shape[1]
    half = BLOCK // 2

    @pl.when(step == 0)
    def _():
        for bank in banks:
            bank[...] = jnp.zeros_like(bank)
        values = table_ref[...].astype(jnp.float32)
        if mirrored:
            blank = jnp.zeros_like(values)
            near_ref[0] = jnp.concatenate([values, blank], axis=2)
            near_ref[1] = jnp.concatenate([blank, values], axis=2)
        else:
            blank = jnp.zeros(values.shape[:2] + (LANES - unknowns,), jnp.float32)
            near_ref[0] = jnp.concatenate([values, blank], axis=2)

    base = step * BLOCK
    empty = jnp.zeros((NRHS, LANES), jnp.float32)

    def operand(k, place):
        if mirrored:
            return near_ref[place // 2, pick_s[k]] * flag_s[k].astype(jnp.float32)
        x = near_ref[0, pick_s[k]]
        return jnp.concatenate([empty, x] if place % 2 else [x, empty], axis=1)

    def group(g, carry):
        start = pl.multiple_of(g * (UNROLL // 2), UNROLL // 2)
        for u in range(0, UNROLL // 2, 2):
            k = base + start + u
            members = (k, k + half, k + 1, k + 1 + half)
            rows = jnp.concatenate([operand(m, n) for n, m in enumerate(members)], axis=0)
            stacked = pairs_ref[pl.ds(start + u, 2)].reshape(2 * unknowns, 2 * LANES)
            dims = (((1,), (0 if mirrored else 1,)), ((), ()))
            product = lax.dot_general(
                rows.astype(jnp.bfloat16), stacked, dims, preferred_element_type=jnp.float32
            )
            for n, m in enumerate(members):
                part = product[n * NRHS:(n + 1) * NRHS]
                if mirrored:
                    part = part[:, (n % 2) * LANES:(n % 2 + 1) * LANES]
                else:
                    part = part[:, :banks[n].shape[2]]
                banks[n][put_s[m]] += part
        return carry

    lax.fori_loop(0, BLOCK // UNROLL, group, 0)

    @pl.when(step == pl.num_programs(0) - 1)
    def _():
        low, high = banks[0][...] + banks[1][...], banks[2][...] + banks[3][...]
        if mirrored:
            out_ref[...] = (low + high)[:, :, :unknowns]
        else:
            out_ref[...] = low[:, :, :unknowns] + high[:, :, unknowns:]


def tile_pass(mirrored, pick, put, flag, pairs, table, rows):
    count, unknowns = 2 * pairs.shape[0], pairs.shape[1]
    near = (2, table.shape[0], NRHS, 2 * unknowns) if mirrored else (1, table.shape[0], NRHS, LANES)
    widths = (LANES,) * BANKS if mirrored else (LANES, LANES, 2 * unknowns, 2 * unknowns)
    return pl.pallas_call(
        functools.partial(pass_kernel, mirrored),
        out_shape=jax.ShapeDtypeStruct((rows, NRHS, unknowns), jnp.float32),
        grid_spec=pltpu.PrefetchScalarGridSpec(
            num_scalar_prefetch=3,
            grid=(count // BLOCK,),
            in_specs=[
                pl.BlockSpec((BLOCK // 2, unknowns, 2 * LANES), lambda s, *_: (s, 0, 0)),
                pl.BlockSpec(table.shape, lambda s, *_: (0, 0, 0)),
            ],
            out_specs=pl.BlockSpec((rows, NRHS, unknowns), lambda s, *_: (0, 0, 0)),
            scratch_shapes=[pltpu.VMEM(near, jnp.float32)]
            + [pltpu.VMEM((rows, NRHS, width), jnp.float32) for width in widths],
        ),
        compiler_params=pltpu.CompilerParams(vmem_limit_bytes=48 * 2**20),
        cost_estimate=pl.CostEstimate(
            flops=2 * count * NRHS * unknowns * unknowns,
            bytes_accessed=2 * count * unknowns * LANES,
            transcendentals=0,
        ),
        name="mirror_pass" if mirrored else "direct_pass",
    )(pick, put, flag, pairs, table)


def gather_kernel(row_s, from_ref, out_ref, wide_ref):
    wide_ref[...] = from_ref[...].astype(jnp.float32)
    send_rows(row_s, wide_ref, out_ref)


def send_rows(row_s, wide_ref, out_ref):
    def group(g, carry):
        start = pl.multiple_of(g * ROWS, ROWS)
        for u in range(ROWS):
            out_ref[start + u] = wide_ref[row_s[start + u]].astype(out_ref.dtype)
        return carry

    lax.fori_loop(0, out_ref.shape[0] // ROWS, group, 0)


def gather(rows, table):
    vmem = pl.BlockSpec(memory_space=pltpu.VMEM)
    return pl.pallas_call(
        gather_kernel,
        out_shape=jax.ShapeDtypeStruct(rows.shape + table.shape[1:], jnp.bfloat16),
        in_specs=[pl.BlockSpec(memory_space=pltpu.SMEM), vmem],
        out_specs=vmem,
        scratch_shapes=[pltpu.VMEM(table.shape, jnp.float32)],
        compiler_params=pltpu.CompilerParams(vmem_limit_bytes=32 * 2**20),
        name="gather_rows",
    )(rows, table)


def combine_kernel(row_s, own_ref, got_ref, out_ref, *rest):
    banks = rest[-BANKS:]
    banks[0][...] = own_ref[...]
    for bank in banks[1:]:
        bank[...] = jnp.zeros_like(bank)

    def group(g, carry):
        start = pl.multiple_of(g * ROWS, ROWS)
        for u in range(ROWS):
            banks[u % BANKS][row_s[start + u]] += got_ref[start + u]
        return carry

    lax.fori_loop(0, got_ref.shape[0] // ROWS, group, 0)
    total = banks[0][...]
    for bank in banks[1:]:
        total += bank[...]
    out_ref[...] = total.astype(out_ref.dtype)
    if len(rest) > BANKS:
        banks[0][...] = total
        send_rows(row_s, banks[0], rest[0])


def combine(rows, own, got, send):
    vmem = pl.BlockSpec(memory_space=pltpu.VMEM)
    out = [jax.ShapeDtypeStruct(own.shape, jnp.bfloat16)]
    if send:
        out.append(jax.ShapeDtypeStruct(got.shape, jnp.bfloat16))
    return pl.pallas_call(
        combine_kernel,
        out_shape=out,
        in_specs=[pl.BlockSpec(memory_space=pltpu.SMEM), vmem, vmem],
        out_specs=[vmem] * len(out),
        scratch_shapes=[pltpu.VMEM(own.shape, jnp.float32)] * BANKS,
        compiler_params=pltpu.CompilerParams(vmem_limit_bytes=32 * 2**20),
        name="combine_rows",
    )(rows, own, got)


def per_device(forces, tiles, tile_local, tile_slot, tile_flag, want_list):
    peers = lax.axis_size("row")
    fibres, width = forces.shape
    unknowns = tiles.shape[1]
    capacity = want_list.shape[2]
    slots = peers * capacity
    wanted = want_list[0]
    everyone = lax.all_gather(wanted, "row", axis=0)
    asked = lax.dynamic_index_in_dim(everyone, lax.axis_index("row"), 1, False).reshape(-1)
    pairs = pair_tiles(tiles)
    def operate(current, sent, again):
        far = lax.all_to_all(sent, "row", 0, 0, tiled=True)
        slot_part = tile_pass(True, tile_local, tile_slot, tile_flag, pairs, current, slots)
        got = lax.all_to_all(slot_part, "row", 0, 0, tiled=True)
        own_part = tile_pass(False, tile_slot, tile_local, tile_flag, pairs, far, fibres)
        return combine(asked, own_part, got, again)

    start = forces.reshape(fibres, NRHS, unknowns)
    one, sent = operate(start, gather(asked, start), True)
    (two,) = operate(one, sent, False)
    return (one.reshape(fibres, width), two.reshape(fibres, width))


def solution(mesh):
    in_specs = (
        P(("groups", "row"), None),
        P(("groups", "row"), None, None),
        P(("groups", "row")),
        P(("groups", "row")),
        P(("groups", "row")),
        P(("groups", "row"), None, None),
    )
    out_specs = (P(("groups", "row"), None), P(("groups", "row"), None))
    return jax.shard_map(
        per_device, mesh=mesh, in_specs=in_specs, out_specs=out_specs, check_vma=False
    )
```

```python
import functools

import jax
import jax.numpy as jnp
from jax import lax
from jax.experimental import pallas as pl
from jax.experimental.pallas import tpu as pltpu
from jax.sharding import PartitionSpec as P

NRHS = 8
BANKS = 4
UNROLL = 64
LANES = 128
ROWS = 16
BLOCK = 128
PITCH = BLOCK + 8


def pair_kernel(tiles_ref, out_ref, turned_ref):
    unknowns = tiles_ref.shape[0]
    half = BLOCK // 2
    blank = jnp.zeros((LANES - unknowns, BLOCK), tiles_ref.dtype)

    def turn(g, carry):
        for u in range(8):
            i = g * 8 + u
            turned = jnp.concatenate([tiles_ref[i], blank], axis=0).T
            turned_ref[pl.ds(pl.multiple_of(i * PITCH, 8), BLOCK), :] = turned.astype(jnp.float32)
        return carry

    lax.fori_loop(0, unknowns // 8, turn, 0)

    def place(g, carry):
        for u in range(4):
            p = g * 4 + u
            low = turned_ref[pl.ds(p, unknowns, stride=PITCH), :]
            high = turned_ref[pl.ds(p + half, unknowns, stride=PITCH), :]
            out_ref[p] = jnp.concatenate([low, high], axis=1).astype(out_ref.dtype)
        return carry

    lax.fori_loop(0, half // 4, place, 0)


def pair_tiles(tiles):
    count, unknowns = tiles.shape[0], tiles.shape[1]
    return pl.pallas_call(
        pair_kernel,
        out_shape=jax.ShapeDtypeStruct((count // 2, unknowns, 2 * LANES), tiles.dtype),
        grid=(count // BLOCK,),
        in_specs=[pl.BlockSpec((unknowns, unknowns, BLOCK), lambda s: (0, 0, s))],
        out_specs=pl.BlockSpec((BLOCK // 2, unknowns, 2 * LANES), lambda s: (s, 0, 0)),
        scratch_shapes=[pltpu.VMEM((unknowns * PITCH, LANES), jnp.float32)],
        compiler_params=pltpu.CompilerParams(vmem_limit_bytes=48 * 2**20),
        cost_estimate=pl.CostEstimate(flops=0, bytes_accessed=44 * 2**20, transcendentals=0),
        name="pair_tiles",
    )(jnp.transpose(tiles, (1, 2, 0)))


def pass_kernel(mirrored, pick_s, put_s, flag_s, pairs_ref, table_ref, out_ref, near_ref, *banks):
    step = pl.program_id(0)
    unknowns = pairs_ref.shape[1]
    half = BLOCK // 2

    @pl.when(step == 0)
    def _():
        for bank in banks:
            bank[...] = jnp.zeros_like(bank)
        values = table_ref[...].astype(jnp.float32)
        if mirrored:
            blank = jnp.zeros_like(values)
            near_ref[0] = jnp.concatenate([values, blank], axis=2)
            near_ref[1] = jnp.concatenate([blank, values], axis=2)
        else:
            blank = jnp.zeros(values.shape[:2] + (LANES - unknowns,), jnp.float32)
            near_ref[0] = jnp.concatenate([values, blank], axis=2)

    base = step * BLOCK
    empty = jnp.zeros((NRHS, LANES), jnp.float32)

    def operand(k, place):
        if mirrored:
            return near_ref[place // 2, pick_s[k]] * flag_s[k].astype(jnp.float32)
        x = near_ref[0, pick_s[k]]
        return jnp.concatenate([empty, x] if place % 2 else [x, empty], axis=1)

    def group(g, carry):
        start = pl.multiple_of(g * (UNROLL // 2), UNROLL // 2)
        for u in range(0, UNROLL // 2, 2):
            k = base + start + u
            members = (k, k + half, k + 1, k + 1 + half)
            rows = jnp.concatenate([operand(m, n) for n, m in enumerate(members)], axis=0)
            stacked = pairs_ref[pl.ds(start + u, 2)].reshape(2 * unknowns, 2 * LANES)
            dims = (((1,), (0 if mirrored else 1,)), ((), ()))
            product = lax.dot_general(
                rows.astype(jnp.bfloat16), stacked, dims, preferred_element_type=jnp.float32
            )
            for n, m in enumerate(members):
                part = product[n * NRHS:(n + 1) * NRHS]
                if mirrored:
                    part = part[:, (n % 2) * LANES:(n % 2 + 1) * LANES]
                else:
                    part = part[:, :banks[n].shape[2]]
                banks[n][put_s[m]] += part
        return carry

    lax.fori_loop(0, BLOCK // UNROLL, group, 0)

    @pl.when(step == pl.num_programs(0) - 1)
    def _():
        low, high = banks[0][...] + banks[1][...], banks[2][...] + banks[3][...]
        if mirrored:
            out_ref[...] = (low + high)[:, :, :unknowns]
        else:
            out_ref[...] = low[:, :, :unknowns] + high[:, :, unknowns:]


def tile_pass(mirrored, pick, put, flag, pairs, table, rows):
    count, unknowns = 2 * pairs.shape[0], pairs.shape[1]
    near = (2, table.shape[0], NRHS, 2 * unknowns) if mirrored else (1, table.shape[0], NRHS, LANES)
    widths = (LANES,) * BANKS if mirrored else (LANES, LANES, 2 * unknowns, 2 * unknowns)
    return pl.pallas_call(
        functools.partial(pass_kernel, mirrored),
        out_shape=jax.ShapeDtypeStruct((rows, NRHS, unknowns), jnp.float32),
        grid_spec=pltpu.PrefetchScalarGridSpec(
            num_scalar_prefetch=3,
            grid=(count // BLOCK,),
            in_specs=[
                pl.BlockSpec((BLOCK // 2, unknowns, 2 * LANES), lambda s, *_: (s, 0, 0)),
                pl.BlockSpec(table.shape, lambda s, *_: (0, 0, 0)),
            ],
            out_specs=pl.BlockSpec((rows, NRHS, unknowns), lambda s, *_: (0, 0, 0)),
            scratch_shapes=[pltpu.VMEM(near, jnp.float32)]
            + [pltpu.VMEM((rows, NRHS, width), jnp.float32) for width in widths],
        ),
        compiler_params=pltpu.CompilerParams(vmem_limit_bytes=48 * 2**20),
        cost_estimate=pl.CostEstimate(
            flops=2 * count * NRHS * unknowns * unknowns,
            bytes_accessed=2 * count * unknowns * LANES,
            transcendentals=0,
        ),
        name="mirror_pass" if mirrored else "direct_pass",
    )(pick, put, flag, pairs, table)


def gather_kernel(row_s, from_ref, out_ref, wide_ref):
    wide_ref[...] = from_ref[...].astype(jnp.float32)
    send_rows(row_s, wide_ref, out_ref)


def send_rows(row_s, wide_ref, out_ref):
    def group(g, carry):
        start = pl.multiple_of(g * ROWS, ROWS)
        for u in range(ROWS):
            out_ref[start + u] = wide_ref[row_s[start + u]].astype(out_ref.dtype)
        return carry

    lax.fori_loop(0, out_ref.shape[0] // ROWS, group, 0)


def gather(rows, table):
    vmem = pl.BlockSpec(memory_space=pltpu.VMEM)
    return pl.pallas_call(
        gather_kernel,
        out_shape=jax.ShapeDtypeStruct(rows.shape + table.shape[1:], jnp.bfloat16),
        in_specs=[pl.BlockSpec(memory_space=pltpu.SMEM), vmem],
        out_specs=vmem,
        scratch_shapes=[pltpu.VMEM(table.shape, jnp.float32)],
        compiler_params=pltpu.CompilerParams(vmem_limit_bytes=32 * 2**20),
        name="gather_rows",
    )(rows, table)


def combine_kernel(row_s, own_ref, got_ref, out_ref, *rest):
    banks = rest[-BANKS:]
    banks[0][...] = own_ref[...]
    for bank in banks[1:]:
        bank[...] = jnp.zeros_like(bank)

    def group(g, carry):
        start = pl.multiple_of(g * ROWS, ROWS)
        for u in range(ROWS):
            banks[u % BANKS][row_s[start + u]] += got_ref[start + u]
        return carry

    lax.fori_loop(0, got_ref.shape[0] // ROWS, group, 0)
    total = banks[0][...]
    for bank in banks[1:]:
        total += bank[...]
    out_ref[...] = total.astype(out_ref.dtype)
    if len(rest) > BANKS:
        banks[0][...] = total
        send_rows(row_s, banks[0], rest[0])


def combine(rows, own, got, send):
    vmem = pl.BlockSpec(memory_space=pltpu.VMEM)
    out = [jax.ShapeDtypeStruct(own.shape, jnp.bfloat16)]
    if send:
        out.append(jax.ShapeDtypeStruct(got.shape, jnp.bfloat16))
    return pl.pallas_call(
        combine_kernel,
        out_shape=out,
        in_specs=[pl.BlockSpec(memory_space=pltpu.SMEM), vmem, vmem],
        out_specs=[vmem] * len(out),
        scratch_shapes=[pltpu.VMEM(own.shape, jnp.float32)] * BANKS,
        compiler_params=pltpu.CompilerParams(vmem_limit_bytes=32 * 2**20),
        name="combine_rows",
    )(rows, own, got)


def per_device(forces, tiles, tile_local, tile_slot, tile_flag, want_list):
    peers = lax.axis_size("row")
    fibres, width = forces.shape
    unknowns = tiles.shape[1]
    capacity = want_list.shape[2]
    slots = peers * capacity
    wanted = want_list[0]
    asked = lax.all_to_all(wanted, "row", 0, 0, tiled=True)
    asked, pairs = lax.optimization_barrier((asked, pair_tiles(tiles)))
    asked = asked.reshape(-1)
    def operate(current, sent, again):
        far = lax.all_to_all(sent, "row", 0, 0, tiled=True)
        slot_part = tile_pass(True, tile_local, tile_slot, tile_flag, pairs, current, slots)
        got = lax.all_to_all(slot_part, "row", 0, 0, tiled=True)
        own_part = tile_pass(False, tile_slot, tile_local, tile_flag, pairs, far, fibres)
        return combine(asked, own_part, got, again)

    start = forces.reshape(fibres, NRHS, unknowns)
    one, sent = operate(start, gather(asked, start), True)
    (two,) = operate(one, sent, False)
    return (one.reshape(fibres, width), two.reshape(fibres, width))


def solution(mesh):
    in_specs = (
        P(("groups", "row"), None),
        P(("groups", "row"), None, None),
        P(("groups", "row")),
        P(("groups", "row")),
        P(("groups", "row")),
        P(("groups", "row"), None, None),
    )
    out_specs = (P(("groups", "row"), None), P(("groups", "row"), None))
    return jax.shard_map(
        per_device, mesh=mesh, in_specs=in_specs, out_specs=out_specs, check_vma=False
    )
```

```python
import functools

import jax
import jax.numpy as jnp
from jax import lax
from jax.experimental import pallas as pl
from jax.experimental.pallas import tpu as pltpu
from jax.sharding import PartitionSpec as P

NRHS = 8
BANKS = 4
UNROLL = 64
LANES = 128
ROWS = 16
BLOCK = 128
PITCH = BLOCK + 8


def pair_kernel(tiles_ref, out_ref, turned_ref):
    unknowns = tiles_ref.shape[0]
    half = BLOCK // 2
    blank = jnp.zeros((LANES - unknowns, BLOCK), tiles_ref.dtype)

    def turn(g, carry):
        for u in range(8):
            i = g * 8 + u
            turned = jnp.concatenate([tiles_ref[i], blank], axis=0).T
            turned_ref[pl.ds(pl.multiple_of(i * PITCH, 8), BLOCK), :] = turned.astype(jnp.float32)
        return carry

    lax.fori_loop(0, unknowns // 8, turn, 0)

    def place(g, carry):
        for u in range(4):
            p = g * 4 + u
            low = turned_ref[pl.ds(p, unknowns, stride=PITCH), :]
            high = turned_ref[pl.ds(p + half, unknowns, stride=PITCH), :]
            out_ref[p] = jnp.concatenate([low, high], axis=1).astype(out_ref.dtype)
        return carry

    lax.fori_loop(0, half // 4, place, 0)


def pair_tiles(tiles):
    count, unknowns = tiles.shape[0], tiles.shape[1]
    return pl.pallas_call(
        pair_kernel,
        out_shape=jax.ShapeDtypeStruct((count // 2, unknowns, 2 * LANES), tiles.dtype),
        grid=(count // BLOCK,),
        in_specs=[pl.BlockSpec((unknowns, unknowns, BLOCK), lambda s: (0, 0, s))],
        out_specs=pl.BlockSpec((BLOCK // 2, unknowns, 2 * LANES), lambda s: (s, 0, 0)),
        scratch_shapes=[pltpu.VMEM((unknowns * PITCH, LANES), jnp.float32)],
        compiler_params=pltpu.CompilerParams(vmem_limit_bytes=48 * 2**20),
        cost_estimate=pl.CostEstimate(flops=0, bytes_accessed=44 * 2**20, transcendentals=0),
        name="pair_tiles",
    )(jnp.transpose(tiles, (1, 2, 0)))


def pack_slots(banks, out_ref, unknowns, capacity):
    piece = LANES - unknowns
    share = unknowns // piece
    kept = capacity * share // (share + 1)

    def peer(p, carry):
        rows = pl.ds(p * capacity, capacity)
        total = (banks[0][rows] + banks[1][rows]) + (banks[2][rows] + banks[3][rows])
        spread = [
            total[kept + m // share][:, (m % share) * piece:(m % share + 1) * piece]
            for m in range(kept)
        ]
        out_ref[pl.ds(p * kept, kept)] = jnp.concatenate(
            [total[:kept, :, :unknowns], jnp.stack(spread)], axis=2
        )
        return carry

    lax.fori_loop(0, out_ref.shape[0] // kept, peer, 0)


def pass_kernel(mirrored, capacity, pick_s, put_s, flag_s, pairs_ref, table_ref, out_ref, near_ref, *banks):
    step = pl.program_id(0)
    unknowns = pairs_ref.shape[1]
    half = BLOCK // 2

    @pl.when(step == 0)
    def _():
        for bank in banks:
            bank[...] = jnp.zeros_like(bank)
        values = table_ref[...].astype(jnp.float32)
        if mirrored:
            blank = jnp.zeros_like(values)
            near_ref[0] = jnp.concatenate([values, blank], axis=2)
            near_ref[1] = jnp.concatenate([blank, values], axis=2)
        else:
            blank = jnp.zeros(values.shape[:2] + (LANES - unknowns,), jnp.float32)
            near_ref[0] = jnp.concatenate([values, blank], axis=2)

    base = step * BLOCK
    empty = jnp.zeros((NRHS, LANES), jnp.float32)

    def operand(k, place):
        if mirrored:
            return near_ref[place // 2, pick_s[k]] * flag_s[k].astype(jnp.float32)
        x = near_ref[0, pick_s[k]]
        return jnp.concatenate([empty, x] if place % 2 else [x, empty], axis=1)

    def group(g, carry):
        start = pl.multiple_of(g * (UNROLL // 2), UNROLL // 2)
        for u in range(0, UNROLL // 2, 2):
            k = base + start + u
            members = (k, k + half, k + 1, k + 1 + half)
            rows = jnp.concatenate([operand(m, n) for n, m in enumerate(members)], axis=0)
            stacked = pairs_ref[pl.ds(start + u, 2)].reshape(2 * unknowns, 2 * LANES)
            dims = (((1,), (0 if mirrored else 1,)), ((), ()))
            product = lax.dot_general(
                rows.astype(jnp.bfloat16), stacked, dims, preferred_element_type=jnp.float32
            )
            for n, m in enumerate(members):
                part = product[n * NRHS:(n + 1) * NRHS]
                if mirrored:
                    part = part[:, (n % 2) * LANES:(n % 2 + 1) * LANES]
                else:
                    part = part[:, :banks[n].shape[2]]
                banks[n][put_s[m]] += part
        return carry

    lax.fori_loop(0, BLOCK // UNROLL, group, 0)

    @pl.when(step == pl.num_programs(0) - 1)
    def _():
        if mirrored:
            pack_slots(banks, out_ref, unknowns, capacity)
        else:
            low, high = banks[0][...] + banks[1][...], banks[2][...] + banks[3][...]
            out_ref[...] = low[:, :, :unknowns] + high[:, :, unknowns:]


def tile_pass(mirrored, pick, put, flag, pairs, table, rows, capacity):
    count, unknowns = 2 * pairs.shape[0], pairs.shape[1]
    near = (2, table.shape[0], NRHS, 2 * unknowns) if mirrored else (1, table.shape[0], NRHS, LANES)
    widths = (LANES,) * BANKS if mirrored else (LANES, LANES, 2 * unknowns, 2 * unknowns)
    if mirrored:
        out = (rows * unknowns // LANES, NRHS, LANES)
    else:
        out = (rows, NRHS, unknowns)
    return pl.pallas_call(
        functools.partial(pass_kernel, mirrored, capacity),
        out_shape=jax.ShapeDtypeStruct(out, jnp.float32),
        grid_spec=pltpu.PrefetchScalarGridSpec(
            num_scalar_prefetch=3,
            grid=(count // BLOCK,),
            in_specs=[
                pl.BlockSpec((BLOCK // 2, unknowns, 2 * LANES), lambda s, *_: (s, 0, 0)),
                pl.BlockSpec(table.shape, lambda s, *_: (0, 0, 0)),
            ],
            out_specs=pl.BlockSpec(out, lambda s, *_: (0, 0, 0)),
            scratch_shapes=[pltpu.VMEM(near, jnp.float32)]
            + [pltpu.VMEM((rows, NRHS, width), jnp.float32) for width in widths],
        ),
        compiler_params=pltpu.CompilerParams(vmem_limit_bytes=48 * 2**20),
        cost_estimate=pl.CostEstimate(
            flops=2 * count * NRHS * unknowns * unknowns,
            bytes_accessed=2 * count * unknowns * LANES,
            transcendentals=0,
        ),
        name="mirror_pass" if mirrored else "direct_pass",
    )(pick, put, flag, pairs, table)


def gather_kernel(row_s, from_ref, out_ref, wide_ref):
    wide_ref[...] = from_ref[...].astype(jnp.float32)
    send_rows(row_s, wide_ref, out_ref)


def send_rows(row_s, wide_ref, out_ref):
    def group(g, carry):
        start = pl.multiple_of(g * ROWS, ROWS)
        for u in range(ROWS):
            out_ref[start + u] = wide_ref[row_s[start + u]].astype(out_ref.dtype)
        return carry

    lax.fori_loop(0, out_ref.shape[0] // ROWS, group, 0)


def gather(rows, table):
    vmem = pl.BlockSpec(memory_space=pltpu.VMEM)
    return pl.pallas_call(
        gather_kernel,
        out_shape=jax.ShapeDtypeStruct(rows.shape + table.shape[1:], jnp.bfloat16),
        in_specs=[pl.BlockSpec(memory_space=pltpu.SMEM), vmem],
        out_specs=vmem,
        scratch_shapes=[pltpu.VMEM(table.shape, jnp.float32)],
        compiler_params=pltpu.CompilerParams(vmem_limit_bytes=32 * 2**20),
        name="gather_rows",
    )(rows, table)


def combine_kernel(capacity, row_s, own_ref, got_ref, out_ref, *rest):
    banks = rest[-BANKS:]
    banks[0][...] = own_ref[...]
    for bank in banks[1:]:
        bank[...] = jnp.zeros_like(bank)

    unknowns = own_ref.shape[2]
    piece = LANES - unknowns
    share = unknowns // piece
    kept = capacity * share // (share + 1)

    def peer(p, carry):
        for c in range(capacity):
            if c < kept:
                got = got_ref[p * kept + c][:, :unknowns]
            else:
                first = p * kept + (c - kept) * share
                got = jnp.concatenate([got_ref[first + t][:, unknowns:] for t in range(share)], axis=1)
            banks[c % BANKS][row_s[p * capacity + c]] += got
        return carry

    lax.fori_loop(0, got_ref.shape[0] // kept, peer, 0)
    total = banks[0][...]
    for bank in banks[1:]:
        total += bank[...]
    out_ref[...] = total.astype(out_ref.dtype)
    if len(rest) > BANKS:
        banks[0][...] = total
        send_rows(row_s, banks[0], rest[0])


def combine(rows, own, got, capacity, send):
    vmem = pl.BlockSpec(memory_space=pltpu.VMEM)
    out = [jax.ShapeDtypeStruct(own.shape, jnp.bfloat16)]
    if send:
        out.append(jax.ShapeDtypeStruct(rows.shape + own.shape[1:], jnp.bfloat16))
    return pl.pallas_call(
        functools.partial(combine_kernel, capacity),
        out_shape=out,
        in_specs=[pl.BlockSpec(memory_space=pltpu.SMEM), vmem, vmem],
        out_specs=[vmem] * len(out),
        scratch_shapes=[pltpu.VMEM(own.shape, jnp.float32)] * BANKS,
        compiler_params=pltpu.CompilerParams(vmem_limit_bytes=32 * 2**20),
        name="combine_rows",
    )(rows, own, got)


def per_device(forces, tiles, tile_local, tile_slot, tile_flag, want_list):
    peers = lax.axis_size("row")
    fibres, width = forces.shape
    unknowns = tiles.shape[1]
    capacity = want_list.shape[2]
    slots = peers * capacity
    wanted = want_list[0]
    asked = lax.all_to_all(wanted, "row", 0, 0, tiled=True)
    asked, pairs = lax.optimization_barrier((asked, pair_tiles(tiles)))
    asked = asked.reshape(-1)
    def operate(current, sent, again):
        far = lax.all_to_all(sent, "row", 0, 0, tiled=True)
        slot_part = tile_pass(True, tile_local, tile_slot, tile_flag, pairs, current, slots, capacity)
        got = lax.all_to_all(slot_part, "row", 0, 0, tiled=True)
        own_part = tile_pass(False, tile_slot, tile_local, tile_flag, pairs, far, fibres, capacity)
        return combine(asked, own_part, got, capacity, again)

    start = forces.reshape(fibres, NRHS, unknowns)
    one, sent = operate(start, gather(asked, start), True)
    (two,) = operate(one, sent, False)
    return (one.reshape(fibres, width), two.reshape(fibres, width))


def solution(mesh):
    in_specs = (
        P(("groups", "row"), None),
        P(("groups", "row"), None, None),
        P(("groups", "row")),
        P(("groups", "row")),
        P(("groups", "row")),
        P(("groups", "row"), None, None),
    )
    out_specs = (P(("groups", "row"), None), P(("groups", "row"), None))
    return jax.shard_map(
        per_device, mesh=mesh, in_specs=in_specs, out_specs=out_specs, check_vma=False
    )
```

```python
import functools

import jax
import jax.numpy as jnp
from jax import lax
from jax.experimental import pallas as pl
from jax.experimental.pallas import tpu as pltpu
from jax.sharding import PartitionSpec as P

NRHS = 8
BANKS = 4
UNROLL = 64
LANES = 128
ROWS = 16
BLOCK = 128
PITCH = BLOCK + 8


def turn_row(i, tiles_ref, turned_ref):
    blank = jnp.zeros((LANES - tiles_ref.shape[1], BLOCK), tiles_ref.dtype)
    turned = jnp.concatenate([tiles_ref[i], blank], axis=0).T
    turned_ref[pl.ds(pl.multiple_of(i * PITCH, 8), BLOCK), :] = turned.astype(jnp.float32)


def place_pairs(turned_ref, out_refs):
    half, unknowns = out_refs[0].shape[0], out_refs[0].shape[1]

    def place(g, carry):
        for u in range(4):
            p = g * 4 + u
            low = turned_ref[pl.ds(p, unknowns, stride=PITCH), :]
            high = turned_ref[pl.ds(p + half, unknowns, stride=PITCH), :]
            pair = jnp.concatenate([low, high], axis=1).astype(out_refs[0].dtype)
            for ref in out_refs:
                ref[p] = pair
        return carry

    lax.fori_loop(0, half // 4, place, 0)


def pack_slots(banks, out_ref, unknowns, capacity):
    piece = LANES - unknowns
    share = unknowns // piece
    kept = capacity * share // (share + 1)

    def peer(p, carry):
        rows = pl.ds(p * capacity, capacity)
        total = (banks[0][rows] + banks[1][rows]) + (banks[2][rows] + banks[3][rows])
        spread = [
            total[kept + m // share][:, (m % share) * piece:(m % share + 1) * piece]
            for m in range(kept)
        ]
        out_ref[pl.ds(p * kept, kept)] = jnp.concatenate(
            [total[:kept, :, :unknowns], jnp.stack(spread)], axis=2
        )
        return carry

    lax.fori_loop(0, out_ref.shape[0] // kept, peer, 0)


def prepare(mirrored, table_ref, near_ref, banks):
    for bank in banks:
        bank[...] = jnp.zeros_like(bank)
    values = table_ref[...].astype(jnp.float32)
    if mirrored:
        blank = jnp.zeros_like(values)
        near_ref[0] = jnp.concatenate([values, blank], axis=2)
        near_ref[1] = jnp.concatenate([blank, values], axis=2)
    else:
        blank = jnp.zeros(values.shape[:2] + (LANES - values.shape[2],), jnp.float32)
        near_ref[0] = jnp.concatenate([values, blank], axis=2)


def apply_four(mirrored, base, p, pick_s, put_s, flag_s, pairs_ref, near_ref, banks):
    half, unknowns = pairs_ref.shape[0], pairs_ref.shape[1]
    empty = jnp.zeros((NRHS, LANES), jnp.float32)

    def operand(k, place):
        if mirrored:
            return near_ref[place // 2, pick_s[k]] * flag_s[k].astype(jnp.float32)
        x = near_ref[0, pick_s[k]]
        return jnp.concatenate([empty, x] if place % 2 else [x, empty], axis=1)

    k = base + p
    members = (k, k + half, k + 1, k + 1 + half)
    rows = jnp.concatenate([operand(m, n) for n, m in enumerate(members)], axis=0)
    stacked = pairs_ref[pl.ds(p, 2)].reshape(2 * unknowns, 2 * LANES)
    dims = (((1,), (0 if mirrored else 1,)), ((), ()))
    product = lax.dot_general(
        rows.astype(jnp.bfloat16), stacked, dims, preferred_element_type=jnp.float32
    )
    for n, m in enumerate(members):
        part = product[n * NRHS:(n + 1) * NRHS]
        if mirrored:
            part = part[:, (n % 2) * LANES:(n % 2 + 1) * LANES]
        else:
            part = part[:, :banks[n].shape[2]]
        banks[n][put_s[m]] += part


def pass_kernel(mirrored, capacity, pick_s, put_s, flag_s, pairs_ref, table_ref, out_ref, near_ref, *banks):
    step = pl.program_id(0)
    unknowns = pairs_ref.shape[1]

    @pl.when(step == 0)
    def _():
        prepare(mirrored, table_ref, near_ref, banks)

    def group(g, carry):
        start = pl.multiple_of(g * (UNROLL // 2), UNROLL // 2)
        for u in range(0, UNROLL // 2, 2):
            apply_four(
                mirrored, step * BLOCK, start + u, pick_s, put_s, flag_s, pairs_ref, near_ref, banks
            )
        return carry

    lax.fori_loop(0, BLOCK // UNROLL, group, 0)

    @pl.when(step == pl.num_programs(0) - 1)
    def _():
        if mirrored:
            pack_slots(banks, out_ref, unknowns, capacity)
        else:
            low, high = banks[0][...] + banks[1][...], banks[2][...] + banks[3][...]
            out_ref[...] = low[:, :, :unknowns] + high[:, :, unknowns:]


def first_kernel(
    capacity, pick_s, put_s, flag_s, tiles_ref, table_ref, pairs_ref, out_ref,
    turned_ref, held_ref, near_ref, *banks
):
    step = pl.program_id(0)
    last = pl.num_programs(0) - 1
    unknowns = tiles_ref.shape[0]
    rounds = 8
    pairs = BLOCK // 2 // rounds

    @pl.when(step == 0)
    def _():
        prepare(True, table_ref, near_ref, banks)

    def work(turning, applying):
        def group(g, carry):
            for u in range(0, pairs, 2):
                if turning:
                    count = 2 * unknowns // rounds // pairs
                    for t in range(count):
                        i = g * (unknowns // rounds) + u // 2 * count + t
                        turn_row(i, tiles_ref, turned_ref)
                if applying:
                    apply_four(
                        True, (step - 1) * BLOCK, g * pairs + u,
                        pick_s, put_s, flag_s, held_ref, near_ref, banks
                    )
            return carry

        lax.fori_loop(0, rounds, group, 0)

    @pl.when(step == 0)
    def _():
        work(True, False)

    @pl.when(jnp.logical_and(step > 0, step < last))
    def _():
        work(True, True)

    @pl.when(step < last)
    def _():
        place_pairs(turned_ref, (pairs_ref, held_ref))

    @pl.when(step == last)
    def _():
        work(False, True)
        pack_slots(banks, out_ref, unknowns, capacity)


def first_pass(pick, put, flag, tiles, table, rows, capacity):
    count, unknowns = tiles.shape[0], tiles.shape[1]
    blocks = count // BLOCK
    out = (rows * unknowns // LANES, NRHS, LANES)
    pair_shape = (BLOCK // 2, unknowns, 2 * LANES)
    return pl.pallas_call(
        functools.partial(first_kernel, capacity),
        out_shape=[
            jax.ShapeDtypeStruct((count // 2,) + pair_shape[1:], tiles.dtype),
            jax.ShapeDtypeStruct(out, jnp.float32),
        ],
        grid_spec=pltpu.PrefetchScalarGridSpec(
            num_scalar_prefetch=3,
            grid=(blocks + 1,),
            in_specs=[
                pl.BlockSpec(
                    (unknowns, unknowns, BLOCK), lambda s, *_: (0, 0, jnp.minimum(s, blocks - 1))
                ),
                pl.BlockSpec(table.shape, lambda s, *_: (0, 0, 0)),
            ],
            out_specs=[
                pl.BlockSpec(pair_shape, lambda s, *_: (jnp.minimum(s, blocks - 1), 0, 0)),
                pl.BlockSpec(out, lambda s, *_: (0, 0, 0)),
            ],
            scratch_shapes=[
                pltpu.VMEM((unknowns * PITCH, LANES), jnp.float32),
                pltpu.VMEM(pair_shape, tiles.dtype),
                pltpu.VMEM((2, table.shape[0], NRHS, 2 * unknowns), jnp.float32),
            ]
            + [pltpu.VMEM((rows, NRHS, LANES), jnp.float32)] * BANKS,
        ),
        compiler_params=pltpu.CompilerParams(vmem_limit_bytes=52 * 2**20),
        cost_estimate=pl.CostEstimate(
            flops=2 * count * NRHS * unknowns * unknowns,
            bytes_accessed=44 * 2**20,
            transcendentals=0,
        ),
        name="pair_and_mirror",
    )(pick, put, flag, jnp.transpose(tiles, (1, 2, 0)), table)


def tile_pass(mirrored, pick, put, flag, pairs, table, rows, capacity):
    count, unknowns = 2 * pairs.shape[0], pairs.shape[1]
    near = (2, table.shape[0], NRHS, 2 * unknowns) if mirrored else (1, table.shape[0], NRHS, LANES)
    widths = (LANES,) * BANKS if mirrored else (LANES, LANES, 2 * unknowns, 2 * unknowns)
    if mirrored:
        out = (rows * unknowns // LANES, NRHS, LANES)
    else:
        out = (rows, NRHS, unknowns)
    return pl.pallas_call(
        functools.partial(pass_kernel, mirrored, capacity),
        out_shape=jax.ShapeDtypeStruct(out, jnp.float32),
        grid_spec=pltpu.PrefetchScalarGridSpec(
            num_scalar_prefetch=3,
            grid=(count // BLOCK,),
            in_specs=[
                pl.BlockSpec((BLOCK // 2, unknowns, 2 * LANES), lambda s, *_: (s, 0, 0)),
                pl.BlockSpec(table.shape, lambda s, *_: (0, 0, 0)),
            ],
            out_specs=pl.BlockSpec(out, lambda s, *_: (0, 0, 0)),
            scratch_shapes=[pltpu.VMEM(near, jnp.float32)]
            + [pltpu.VMEM((rows, NRHS, width), jnp.float32) for width in widths],
        ),
        compiler_params=pltpu.CompilerParams(vmem_limit_bytes=48 * 2**20),
        cost_estimate=pl.CostEstimate(
            flops=2 * count * NRHS * unknowns * unknowns,
            bytes_accessed=2 * count * unknowns * LANES,
            transcendentals=0,
        ),
        name="mirror_pass" if mirrored else "direct_pass",
    )(pick, put, flag, pairs, table)


def gather_kernel(row_s, from_ref, out_ref, wide_ref):
    wide_ref[...] = from_ref[...].astype(jnp.float32)
    send_rows(row_s, wide_ref, out_ref)


def send_rows(row_s, wide_ref, out_ref):
    def group(g, carry):
        start = pl.multiple_of(g * ROWS, ROWS)
        for u in range(ROWS):
            out_ref[start + u] = wide_ref[row_s[start + u]].astype(out_ref.dtype)
        return carry

    lax.fori_loop(0, out_ref.shape[0] // ROWS, group, 0)


def gather(rows, table):
    vmem = pl.BlockSpec(memory_space=pltpu.VMEM)
    return pl.pallas_call(
        gather_kernel,
        out_shape=jax.ShapeDtypeStruct(rows.shape + table.shape[1:], jnp.bfloat16),
        in_specs=[pl.BlockSpec(memory_space=pltpu.SMEM), vmem],
        out_specs=vmem,
        scratch_shapes=[pltpu.VMEM(table.shape, jnp.float32)],
        compiler_params=pltpu.CompilerParams(vmem_limit_bytes=32 * 2**20),
        name="gather_rows",
    )(rows, table)


def combine_kernel(capacity, row_s, own_ref, got_ref, out_ref, *rest):
    banks = rest[-BANKS:]
    banks[0][...] = own_ref[...]
    for bank in banks[1:]:
        bank[...] = jnp.zeros_like(bank)

    unknowns = own_ref.shape[2]
    piece = LANES - unknowns
    share = unknowns // piece
    kept = capacity * share // (share + 1)

    def peer(p, carry):
        for c in range(capacity):
            if c < kept:
                got = got_ref[p * kept + c][:, :unknowns]
            else:
                first = p * kept + (c - kept) * share
                got = jnp.concatenate([got_ref[first + t][:, unknowns:] for t in range(share)], axis=1)
            banks[c % BANKS][row_s[p * capacity + c]] += got
        return carry

    lax.fori_loop(0, got_ref.shape[0] // kept, peer, 0)
    total = banks[0][...]
    for bank in banks[1:]:
        total += bank[...]
    out_ref[...] = total.astype(out_ref.dtype)
    if len(rest) > BANKS:
        banks[0][...] = total
        send_rows(row_s, banks[0], rest[0])


def combine(rows, own, got, capacity, send):
    vmem = pl.BlockSpec(memory_space=pltpu.VMEM)
    out = [jax.ShapeDtypeStruct(own.shape, jnp.bfloat16)]
    if send:
        out.append(jax.ShapeDtypeStruct(rows.shape + own.shape[1:], jnp.bfloat16))
    return pl.pallas_call(
        functools.partial(combine_kernel, capacity),
        out_shape=out,
        in_specs=[pl.BlockSpec(memory_space=pltpu.SMEM), vmem, vmem],
        out_specs=[vmem] * len(out),
        scratch_shapes=[pltpu.VMEM(own.shape, jnp.float32)] * BANKS,
        compiler_params=pltpu.CompilerParams(vmem_limit_bytes=32 * 2**20),
        name="combine_rows",
    )(rows, own, got)


def per_device(forces, tiles, tile_local, tile_slot, tile_flag, want_list):
    peers = lax.axis_size("row")
    fibres, width = forces.shape
    unknowns = tiles.shape[1]
    capacity = want_list.shape[2]
    slots = peers * capacity
    wanted = want_list[0]
    start = forces.reshape(fibres, NRHS, unknowns)
    asked = lax.all_to_all(wanted, "row", 0, 0, tiled=True).reshape(-1)
    first_sent, start = lax.optimization_barrier((gather(asked, start), start))
    pairs, mirrored = first_pass(tile_local, tile_slot, tile_flag, tiles, start, slots, capacity)

    def finish(mirrored, sent, again):
        got = lax.all_to_all(mirrored, "row", 0, 0, tiled=True)
        far = lax.all_to_all(sent, "row", 0, 0, tiled=True)
        own = tile_pass(False, tile_slot, tile_local, tile_flag, pairs, far, fibres, capacity)
        return combine(asked, own, got, capacity, again)

    one, sent = finish(mirrored, first_sent, True)
    mirrored = tile_pass(True, tile_local, tile_slot, tile_flag, pairs, one, slots, capacity)
    (two,) = finish(mirrored, sent, False)
    return (one.reshape(fibres, width), two.reshape(fibres, width))


def solution(mesh):
    in_specs = (
        P(("groups", "row"), None),
        P(("groups", "row"), None, None),
        P(("groups", "row")),
        P(("groups", "row")),
        P(("groups", "row")),
        P(("groups", "row"), None, None),
    )
    out_specs = (P(("groups", "row"), None), P(("groups", "row"), None))
    return jax.shard_map(
        per_device, mesh=mesh, in_specs=in_specs, out_specs=out_specs, check_vma=False
    )
```

```python
import functools

import jax
import jax.numpy as jnp
from jax import lax
from jax.experimental import pallas as pl
from jax.experimental.pallas import tpu as pltpu
from jax.sharding import PartitionSpec as P

NRHS = 8
BANKS = 4
UNROLL = 128
LANES = 128
ROWS = 16
BLOCK = 128
PITCH = BLOCK + 8


def turn_row(i, tiles_ref, turned_ref):
    blank = jnp.zeros((LANES - tiles_ref.shape[1], BLOCK), tiles_ref.dtype)
    turned = jnp.concatenate([tiles_ref[i], blank], axis=0).T
    turned_ref[pl.ds(pl.multiple_of(i * PITCH, 8), BLOCK), :] = turned.astype(jnp.float32)


def place_pairs(turned_ref, out_refs):
    half, unknowns = out_refs[0].shape[0], out_refs[0].shape[1]

    def place(g, carry):
        for u in range(16):
            p = g * 16 + u
            low = turned_ref[pl.ds(p, unknowns, stride=PITCH), :]
            high = turned_ref[pl.ds(p + half, unknowns, stride=PITCH), :]
            pair = jnp.concatenate([low, high], axis=1).astype(out_refs[0].dtype)
            for ref in out_refs:
                ref[p] = pair
        return carry

    lax.fori_loop(0, half // 16, place, 0)


def pack_slots(banks, out_ref, unknowns, capacity):
    piece = LANES - unknowns
    share = unknowns // piece
    kept = capacity * share // (share + 1)

    def peer(p, carry):
        rows = pl.ds(p * capacity, capacity)
        total = (banks[0][rows] + banks[1][rows]) + (banks[2][rows] + banks[3][rows])
        spread = [
            total[kept + m // share][:, (m % share) * piece:(m % share + 1) * piece]
            for m in range(kept)
        ]
        out_ref[pl.ds(p * kept, kept)] = jnp.concatenate(
            [total[:kept, :, :unknowns], jnp.stack(spread)], axis=2
        )
        return carry

    lax.fori_loop(0, out_ref.shape[0] // kept, peer, 0, unroll=4)


def prepare(mirrored, table_ref, near_ref, banks):
    for bank in banks:
        bank[...] = jnp.zeros_like(bank)
    values = table_ref[...].astype(jnp.float32)
    if mirrored:
        blank = jnp.zeros_like(values)
        near_ref[0] = jnp.concatenate([values, blank], axis=2)
        near_ref[1] = jnp.concatenate([blank, values], axis=2)
    else:
        blank = jnp.zeros(values.shape[:2] + (LANES - values.shape[2],), jnp.float32)
        near_ref[0] = jnp.concatenate([values, blank], axis=2)


def apply_four(mirrored, base, p, index_s, pairs_ref, near_ref, banks):
    half, unknowns = pairs_ref.shape[0], pairs_ref.shape[1]
    empty = jnp.zeros((NRHS, LANES), jnp.float32)
    count = index_s.shape[0] // 3

    def operand(k, place):
        if mirrored:
            return near_ref[place // 2, index_s[k]] * index_s[2 * count + k].astype(jnp.float32)
        x = near_ref[0, index_s[count + k]]
        return jnp.concatenate([empty, x] if place % 2 else [x, empty], axis=1)

    k = base + p
    members = (k, k + half, k + 1, k + 1 + half)
    rows = jnp.concatenate([operand(m, n) for n, m in enumerate(members)], axis=0)
    stacked = pairs_ref[pl.ds(p, 2)].reshape(2 * unknowns, 2 * LANES)
    dims = (((1,), (0 if mirrored else 1,)), ((), ()))
    product = lax.dot_general(
        rows.astype(jnp.bfloat16), stacked, dims, preferred_element_type=jnp.float32
    )
    for n, m in enumerate(members):
        part = product[n * NRHS:(n + 1) * NRHS]
        if mirrored:
            part = part[:, (n % 2) * LANES:(n % 2 + 1) * LANES]
        else:
            part = part[:, :banks[n].shape[2]]
        banks[n][index_s[(count if mirrored else 0) + m]] += part


def pass_kernel(mirrored, capacity, index_s, pairs_ref, table_ref, out_ref, near_ref, *banks):
    step = pl.program_id(0)
    unknowns = pairs_ref.shape[1]

    @pl.when(step == 0)
    def _():
        prepare(mirrored, table_ref, near_ref, banks)

    def group(g, carry):
        start = pl.multiple_of(g * (UNROLL // 2), UNROLL // 2)
        for u in range(0, UNROLL // 2, 2):
            apply_four(
                mirrored, step * BLOCK, start + u, index_s, pairs_ref, near_ref, banks
            )
        return carry

    lax.fori_loop(0, BLOCK // UNROLL, group, 0)

    @pl.when(step == pl.num_programs(0) - 1)
    def _():
        if mirrored:
            pack_slots(banks, out_ref, unknowns, capacity)
        else:
            low, high = banks[0][...] + banks[1][...], banks[2][...] + banks[3][...]
            out_ref[...] = low[:, :, :unknowns] + high[:, :, unknowns:]


def first_kernel(
    capacity, index_s, tiles_ref, table_ref, pairs_ref, out_ref,
    turned_ref, held_ref, near_ref, *banks
):
    step = pl.program_id(0)
    last = pl.num_programs(0) - 1
    unknowns = tiles_ref.shape[0]
    rounds = 2
    pairs = BLOCK // 2 // rounds

    @pl.when(step == 0)
    def _():
        prepare(True, table_ref, near_ref, banks)

    def work(turning, applying):
        def group(g, carry):
            for u in range(0, pairs, 2):
                if turning:
                    count = 2 * unknowns // rounds // pairs
                    for t in range(count):
                        i = g * (unknowns // rounds) + u // 2 * count + t
                        turn_row(i, tiles_ref, turned_ref)
                if applying:
                    apply_four(
                        True, (step - 1) * BLOCK, g * pairs + u,
                        index_s, held_ref, near_ref, banks
                    )
            return carry

        lax.fori_loop(0, rounds, group, 0)

    @pl.when(step == 0)
    def _():
        work(True, False)

    @pl.when(jnp.logical_and(step > 0, step < last))
    def _():
        work(True, True)

    @pl.when(step < last)
    def _():
        place_pairs(turned_ref, (pairs_ref, held_ref))

    @pl.when(step == last)
    def _():
        work(False, True)
        pack_slots(banks, out_ref, unknowns, capacity)


def first_pass(index, tiles, table, rows, capacity):
    count, unknowns = tiles.shape[0], tiles.shape[1]
    blocks = count // BLOCK
    out = (rows * unknowns // LANES, NRHS, LANES)
    pair_shape = (BLOCK // 2, unknowns, 2 * LANES)
    return pl.pallas_call(
        functools.partial(first_kernel, capacity),
        out_shape=[
            jax.ShapeDtypeStruct((count // 2,) + pair_shape[1:], tiles.dtype),
            jax.ShapeDtypeStruct(out, jnp.float32),
        ],
        grid_spec=pltpu.PrefetchScalarGridSpec(
            num_scalar_prefetch=1,
            grid=(blocks + 1,),
            in_specs=[
                pl.BlockSpec(
                    (unknowns, unknowns, BLOCK), lambda s, *_: (0, 0, jnp.minimum(s, blocks - 1))
                ),
                pl.BlockSpec(table.shape, lambda s, *_: (0, 0, 0)),
            ],
            out_specs=[
                pl.BlockSpec(pair_shape, lambda s, *_: (jnp.minimum(s, blocks - 1), 0, 0)),
                pl.BlockSpec(out, lambda s, *_: (0, 0, 0)),
            ],
            scratch_shapes=[
                pltpu.VMEM((unknowns * PITCH, LANES), jnp.float32),
                pltpu.VMEM(pair_shape, tiles.dtype),
                pltpu.VMEM((2, table.shape[0], NRHS, 2 * unknowns), jnp.float32),
            ]
            + [pltpu.VMEM((rows, NRHS, LANES), jnp.float32)] * BANKS,
        ),
        compiler_params=pltpu.CompilerParams(vmem_limit_bytes=52 * 2**20),
        cost_estimate=pl.CostEstimate(
            flops=2 * count * NRHS * unknowns * unknowns,
            bytes_accessed=44 * 2**20,
            transcendentals=0,
        ),
        name="pair_and_mirror",
    )(index, jnp.transpose(tiles, (1, 2, 0)), table)


def tile_pass(mirrored, index, pairs, table, rows, capacity):
    count, unknowns = 2 * pairs.shape[0], pairs.shape[1]
    near = (2, table.shape[0], NRHS, 2 * unknowns) if mirrored else (1, table.shape[0], NRHS, LANES)
    widths = (LANES,) * BANKS if mirrored else (LANES, LANES, 2 * unknowns, 2 * unknowns)
    if mirrored:
        out = (rows * unknowns // LANES, NRHS, LANES)
    else:
        out = (rows, NRHS, unknowns)
    return pl.pallas_call(
        functools.partial(pass_kernel, mirrored, capacity),
        out_shape=jax.ShapeDtypeStruct(out, jnp.float32),
        grid_spec=pltpu.PrefetchScalarGridSpec(
            num_scalar_prefetch=1,
            grid=(count // BLOCK,),
            in_specs=[
                pl.BlockSpec((BLOCK // 2, unknowns, 2 * LANES), lambda s, *_: (s, 0, 0)),
                pl.BlockSpec(table.shape, lambda s, *_: (0, 0, 0)),
            ],
            out_specs=pl.BlockSpec(out, lambda s, *_: (0, 0, 0)),
            scratch_shapes=[pltpu.VMEM(near, jnp.float32)]
            + [pltpu.VMEM((rows, NRHS, width), jnp.float32) for width in widths],
        ),
        compiler_params=pltpu.CompilerParams(vmem_limit_bytes=48 * 2**20),
        cost_estimate=pl.CostEstimate(
            flops=2 * count * NRHS * unknowns * unknowns,
            bytes_accessed=2 * count * unknowns * LANES,
            transcendentals=0,
        ),
        name="mirror_pass" if mirrored else "direct_pass",
    )(index, pairs, table)


def gather_kernel(row_s, from_ref, out_ref, wide_ref):
    wide_ref[...] = from_ref[...].astype(jnp.float32)
    send_rows(row_s, wide_ref, out_ref)


def send_rows(row_s, wide_ref, out_ref):
    def group(g, carry):
        start = pl.multiple_of(g * ROWS, ROWS)
        for u in range(ROWS):
            out_ref[start + u] = wide_ref[row_s[start + u]].astype(out_ref.dtype)
        return carry

    lax.fori_loop(0, out_ref.shape[0] // ROWS, group, 0)


def gather(rows, table):
    vmem = pl.BlockSpec(memory_space=pltpu.VMEM)
    return pl.pallas_call(
        gather_kernel,
        out_shape=jax.ShapeDtypeStruct(rows.shape + table.shape[1:], jnp.bfloat16),
        in_specs=[pl.BlockSpec(memory_space=pltpu.SMEM), vmem],
        out_specs=vmem,
        scratch_shapes=[pltpu.VMEM(table.shape, jnp.float32)],
        compiler_params=pltpu.CompilerParams(vmem_limit_bytes=32 * 2**20),
        name="gather_rows",
    )(rows, table)


def combine_kernel(capacity, row_s, own_ref, got_ref, out_ref, *rest):
    banks = rest[-BANKS:]
    banks[0][...] = own_ref[...]
    for bank in banks[1:]:
        bank[...] = jnp.zeros_like(bank)

    unknowns = own_ref.shape[2]
    piece = LANES - unknowns
    share = unknowns // piece
    kept = capacity * share // (share + 1)

    def peer(p, carry):
        for c in range(capacity):
            if c < kept:
                got = got_ref[p * kept + c][:, :unknowns]
            else:
                first = p * kept + (c - kept) * share
                got = jnp.concatenate([got_ref[first + t][:, unknowns:] for t in range(share)], axis=1)
            banks[c % BANKS][row_s[p * capacity + c]] += got
        return carry

    lax.fori_loop(0, got_ref.shape[0] // kept, peer, 0, unroll=4)
    total = banks[0][...]
    for bank in banks[1:]:
        total += bank[...]
    out_ref[...] = total.astype(out_ref.dtype)
    if len(rest) > BANKS:
        banks[0][...] = total
        send_rows(row_s, banks[0], rest[0])


def combine(rows, own, got, capacity, send):
    vmem = pl.BlockSpec(memory_space=pltpu.VMEM)
    out = [jax.ShapeDtypeStruct(own.shape, jnp.bfloat16)]
    if send:
        out.append(jax.ShapeDtypeStruct(rows.shape + own.shape[1:], jnp.bfloat16))
    return pl.pallas_call(
        functools.partial(combine_kernel, capacity),
        out_shape=out,
        in_specs=[pl.BlockSpec(memory_space=pltpu.SMEM), vmem, vmem],
        out_specs=[vmem] * len(out),
        scratch_shapes=[pltpu.VMEM(own.shape, jnp.float32)] * BANKS,
        compiler_params=pltpu.CompilerParams(vmem_limit_bytes=32 * 2**20),
        name="combine_rows",
    )(rows, own, got)


def per_device(forces, tiles, tile_local, tile_slot, tile_flag, want_list):
    peers = lax.axis_size("row")
    fibres, width = forces.shape
    unknowns = tiles.shape[1]
    capacity = want_list.shape[2]
    slots = peers * capacity
    wanted = want_list[0]
    start = forces.reshape(fibres, NRHS, unknowns)
    index = jnp.concatenate([tile_local, tile_slot, tile_flag])
    asked = lax.all_to_all(wanted, "row", 0, 0, tiled=True)
    asked, index = lax.optimization_barrier((asked, index))
    asked = asked.reshape(-1)
    first_sent, start = lax.optimization_barrier((gather(asked, start), start))
    pairs, mirrored = first_pass(index, tiles, start, slots, capacity)

    def finish(mirrored, sent, again):
        got = lax.all_to_all(mirrored, "row", 0, 0, tiled=True)
        far = lax.all_to_all(sent, "row", 0, 0, tiled=True)
        own = tile_pass(False, index, pairs, far, fibres, capacity)
        return combine(asked, own, got, capacity, again)

    one, sent = finish(mirrored, first_sent, True)
    mirrored = tile_pass(True, index, pairs, one, slots, capacity)
    (two,) = finish(mirrored, sent, False)
    return (one.reshape(fibres, width), two.reshape(fibres, width))


def solution(mesh):
    in_specs = (
        P(("groups", "row"), None),
        P(("groups", "row"), None, None),
        P(("groups", "row")),
        P(("groups", "row")),
        P(("groups", "row")),
        P(("groups", "row"), None, None),
    )
    out_specs = (P(("groups", "row"), None), P(("groups", "row"), None))
    return jax.shard_map(
        per_device, mesh=mesh, in_specs=in_specs, out_specs=out_specs, check_vma=False
    )
```

```python
import functools

import jax
import jax.numpy as jnp
from jax import lax
from jax.experimental import pallas as pl
from jax.experimental.pallas import tpu as pltpu
from jax.sharding import PartitionSpec as P

NRHS = 8
BANKS = 4
JOINED = 2
LANES = 128
ROWS = 16
BLOCK = 128
PITCH = BLOCK + 8


def turn_row(i, tiles_ref, turned_ref):
    blank = jnp.zeros((LANES - tiles_ref.shape[1], BLOCK), tiles_ref.dtype)
    turned = jnp.concatenate([tiles_ref[i], blank], axis=0).T
    turned_ref[pl.ds(pl.multiple_of(i * PITCH, 8), BLOCK), :] = turned.astype(jnp.float32)


def place_pairs(turned_ref, out_refs):
    half, unknowns = out_refs[0].shape[0], out_refs[0].shape[1]

    def place(g, carry):
        for u in range(16):
            p = g * 16 + u
            low = turned_ref[pl.ds(p, unknowns, stride=PITCH), :]
            high = turned_ref[pl.ds(p + half, unknowns, stride=PITCH), :]
            pair = jnp.concatenate([low, high], axis=1).astype(out_refs[0].dtype)
            for ref in out_refs:
                ref[p] = pair
        return carry

    lax.fori_loop(0, half // 16, place, 0)


def pack_slots(banks, out_ref, unknowns, capacity):
    piece = LANES - unknowns
    share = unknowns // piece
    kept = capacity * share // (share + 1)

    def peer(p, carry):
        rows = pl.ds(p * capacity, capacity)
        total = (banks[0][rows] + banks[1][rows]) + (banks[2][rows] + banks[3][rows])
        spread = [
            total[kept + m // share][:, (m % share) * piece:(m % share + 1) * piece]
            for m in range(kept)
        ]
        out_ref[pl.ds(p * kept, kept)] = jnp.concatenate(
            [total[:kept, :, :unknowns], jnp.stack(spread)], axis=2
        )
        return carry

    lax.fori_loop(0, out_ref.shape[0] // kept, peer, 0, unroll=4)


def prepare(mirrored, table_ref, near_ref, banks):
    for bank in banks:
        bank[...] = jnp.zeros_like(bank)
    values = table_ref[...].astype(jnp.float32)
    if mirrored:
        blank = jnp.zeros_like(values)
        near_ref[0] = jnp.concatenate([values, blank], axis=2)
        near_ref[1] = jnp.concatenate([blank, values], axis=2)
    else:
        blank = jnp.zeros(values.shape[:2] + (LANES - values.shape[2],), jnp.float32)
        near_ref[0] = jnp.concatenate([values, blank], axis=2)


def apply_four(mirrored, base, p, index_s, pairs_ref, near_ref, banks):
    half, unknowns = pairs_ref.shape[0], pairs_ref.shape[1]
    empty = jnp.zeros((NRHS, LANES), jnp.float32)
    count = index_s.shape[0] // 3

    def operand(k, place):
        if mirrored:
            return near_ref[place // 2, index_s[k]] * index_s[2 * count + k].astype(jnp.float32)
        x = near_ref[0, index_s[count + k]]
        return jnp.concatenate([empty, x] if place % 2 else [x, empty], axis=1)

    k = base + p
    members = (k, k + half, k + 1, k + 1 + half)
    rows = jnp.concatenate([operand(m, n) for n, m in enumerate(members)], axis=0)
    stacked = pairs_ref[pl.ds(p, 2)].reshape(2 * unknowns, 2 * LANES)
    dims = (((1,), (0 if mirrored else 1,)), ((), ()))
    product = lax.dot_general(
        rows.astype(jnp.bfloat16), stacked, dims, preferred_element_type=jnp.float32
    )
    for n, m in enumerate(members):
        part = product[n * NRHS:(n + 1) * NRHS]
        if mirrored:
            part = part[:, (n % 2) * LANES:(n % 2 + 1) * LANES]
        else:
            part = part[:, :banks[n].shape[2]]
        banks[n][index_s[(count if mirrored else 0) + m]] += part


def pass_kernel(mirrored, capacity, index_s, pairs_ref, table_ref, out_ref, near_ref, *banks):
    step = pl.program_id(0)
    unknowns = pairs_ref.shape[1]

    @pl.when(step == 0)
    def _():
        prepare(mirrored, table_ref, near_ref, banks)

    half = BLOCK // 2
    for b in range(JOINED):
        view = pairs_ref.at[pl.ds(b * half, half)]
        for p in range(0, half, 2):
            apply_four(mirrored, (step * JOINED + b) * BLOCK, p, index_s, view, near_ref, banks)

    @pl.when(step == pl.num_programs(0) - 1)
    def _():
        if mirrored:
            pack_slots(banks, out_ref, unknowns, capacity)
        else:
            low, high = banks[0][...] + banks[1][...], banks[2][...] + banks[3][...]
            out_ref[...] = low[:, :, :unknowns] + high[:, :, unknowns:]


def first_kernel(
    capacity, index_s, tiles_ref, table_ref, pairs_ref, out_ref,
    turned_ref, held_ref, near_ref, *banks
):
    step = pl.program_id(0)
    last = pl.num_programs(0) - 1
    unknowns = tiles_ref.shape[0]
    rounds = 1
    pairs = BLOCK // 2 // rounds

    @pl.when(step == 0)
    def _():
        prepare(True, table_ref, near_ref, banks)

    def work(turning, applying):
        def group(g, carry):
            for u in range(0, pairs, 2):
                if turning:
                    count = 2 * unknowns // rounds // pairs
                    for t in range(count):
                        i = g * (unknowns // rounds) + u // 2 * count + t
                        turn_row(i, tiles_ref, turned_ref)
                if applying:
                    apply_four(
                        True, (step - 1) * BLOCK, g * pairs + u,
                        index_s, held_ref, near_ref, banks
                    )
            return carry

        lax.fori_loop(0, rounds, group, 0)

    @pl.when(step == 0)
    def _():
        work(True, False)

    @pl.when(jnp.logical_and(step > 0, step < last))
    def _():
        work(True, True)

    @pl.when(step < last)
    def _():
        place_pairs(turned_ref, (pairs_ref, held_ref))

    @pl.when(step == last)
    def _():
        work(False, True)
        pack_slots(banks, out_ref, unknowns, capacity)


def first_pass(index, tiles, table, rows, capacity):
    count, unknowns = tiles.shape[0], tiles.shape[1]
    blocks = count // BLOCK
    out = (rows * unknowns // LANES, NRHS, LANES)
    pair_shape = (BLOCK // 2, unknowns, 2 * LANES)
    return pl.pallas_call(
        functools.partial(first_kernel, capacity),
        out_shape=[
            jax.ShapeDtypeStruct((count // 2,) + pair_shape[1:], tiles.dtype),
            jax.ShapeDtypeStruct(out, jnp.float32),
        ],
        grid_spec=pltpu.PrefetchScalarGridSpec(
            num_scalar_prefetch=1,
            grid=(blocks + 1,),
            in_specs=[
                pl.BlockSpec(
                    (unknowns, unknowns, BLOCK), lambda s, *_: (0, 0, jnp.minimum(s, blocks - 1))
                ),
                pl.BlockSpec(table.shape, lambda s, *_: (0, 0, 0)),
            ],
            out_specs=[
                pl.BlockSpec(pair_shape, lambda s, *_: (jnp.minimum(s, blocks - 1), 0, 0)),
                pl.BlockSpec(out, lambda s, *_: (0, 0, 0)),
            ],
            scratch_shapes=[
                pltpu.VMEM((unknowns * PITCH, LANES), jnp.float32),
                pltpu.VMEM(pair_shape, tiles.dtype),
                pltpu.VMEM((2, table.shape[0], NRHS, 2 * unknowns), jnp.float32),
            ]
            + [pltpu.VMEM((rows, NRHS, LANES), jnp.float32)] * BANKS,
        ),
        compiler_params=pltpu.CompilerParams(vmem_limit_bytes=52 * 2**20),
        cost_estimate=pl.CostEstimate(
            flops=2 * count * NRHS * unknowns * unknowns,
            bytes_accessed=44 * 2**20,
            transcendentals=0,
        ),
        name="pair_and_mirror",
    )(index, jnp.transpose(tiles, (1, 2, 0)), table)


def tile_pass(mirrored, index, pairs, table, rows, capacity):
    count, unknowns = 2 * pairs.shape[0], pairs.shape[1]
    near = (2, table.shape[0], NRHS, 2 * unknowns) if mirrored else (1, table.shape[0], NRHS, LANES)
    widths = (LANES,) * BANKS if mirrored else (LANES, LANES, 2 * unknowns, 2 * unknowns)
    if mirrored:
        out = (rows * unknowns // LANES, NRHS, LANES)
    else:
        out = (rows, NRHS, unknowns)
    return pl.pallas_call(
        functools.partial(pass_kernel, mirrored, capacity),
        out_shape=jax.ShapeDtypeStruct(out, jnp.float32),
        grid_spec=pltpu.PrefetchScalarGridSpec(
            num_scalar_prefetch=1,
            grid=(count // (JOINED * BLOCK),),
            in_specs=[
                pl.BlockSpec((JOINED * BLOCK // 2, unknowns, 2 * LANES), lambda s, *_: (s, 0, 0)),
                pl.BlockSpec(table.shape, lambda s, *_: (0, 0, 0)),
            ],
            out_specs=pl.BlockSpec(out, lambda s, *_: (0, 0, 0)),
            scratch_shapes=[pltpu.VMEM(near, jnp.float32)]
            + [pltpu.VMEM((rows, NRHS, width), jnp.float32) for width in widths],
        ),
        compiler_params=pltpu.CompilerParams(vmem_limit_bytes=48 * 2**20),
        cost_estimate=pl.CostEstimate(
            flops=2 * count * NRHS * unknowns * unknowns,
            bytes_accessed=2 * count * unknowns * LANES,
            transcendentals=0,
        ),
        name="mirror_pass" if mirrored else "direct_pass",
    )(index, pairs, table)


def gather_kernel(row_s, from_ref, out_ref, wide_ref):
    wide_ref[...] = from_ref[...].astype(jnp.float32)
    send_rows(row_s, wide_ref, out_ref)


def send_rows(row_s, wide_ref, out_ref):
    def group(g, carry):
        start = pl.multiple_of(g * ROWS, ROWS)
        for u in range(ROWS):
            out_ref[start + u] = wide_ref[row_s[start + u]].astype(out_ref.dtype)
        return carry

    lax.fori_loop(0, out_ref.shape[0] // ROWS, group, 0)


def gather(rows, table):
    vmem = pl.BlockSpec(memory_space=pltpu.VMEM)
    return pl.pallas_call(
        gather_kernel,
        out_shape=jax.ShapeDtypeStruct(rows.shape + table.shape[1:], jnp.bfloat16),
        in_specs=[pl.BlockSpec(memory_space=pltpu.SMEM), vmem],
        out_specs=vmem,
        scratch_shapes=[pltpu.VMEM(table.shape, jnp.float32)],
        compiler_params=pltpu.CompilerParams(vmem_limit_bytes=32 * 2**20),
        name="gather_rows",
    )(rows, table)


def combine_kernel(capacity, row_s, own_ref, got_ref, out_ref, *rest):
    banks = rest[-BANKS:]
    banks[0][...] = own_ref[...]
    for bank in banks[1:]:
        bank[...] = jnp.zeros_like(bank)

    unknowns = own_ref.shape[2]
    piece = LANES - unknowns
    share = unknowns // piece
    kept = capacity * share // (share + 1)

    def peer(p, carry):
        for c in range(capacity):
            if c < kept:
                got = got_ref[p * kept + c][:, :unknowns]
            else:
                first = p * kept + (c - kept) * share
                got = jnp.concatenate([got_ref[first + t][:, unknowns:] for t in range(share)], axis=1)
            banks[c % BANKS][row_s[p * capacity + c]] += got
        return carry

    lax.fori_loop(0, got_ref.shape[0] // kept, peer, 0, unroll=4)
    total = banks[0][...]
    for bank in banks[1:]:
        total += bank[...]
    out_ref[...] = total.astype(out_ref.dtype)
    if len(rest) > BANKS:
        banks[0][...] = total
        send_rows(row_s, banks[0], rest[0])


def combine(rows, own, got, capacity, send):
    vmem = pl.BlockSpec(memory_space=pltpu.VMEM)
    out = [jax.ShapeDtypeStruct(own.shape, jnp.bfloat16)]
    if send:
        out.append(jax.ShapeDtypeStruct(rows.shape + own.shape[1:], jnp.bfloat16))
    return pl.pallas_call(
        functools.partial(combine_kernel, capacity),
        out_shape=out,
        in_specs=[pl.BlockSpec(memory_space=pltpu.SMEM), vmem, vmem],
        out_specs=[vmem] * len(out),
        scratch_shapes=[pltpu.VMEM(own.shape, jnp.float32)] * BANKS,
        compiler_params=pltpu.CompilerParams(vmem_limit_bytes=32 * 2**20),
        name="combine_rows",
    )(rows, own, got)


def per_device(forces, tiles, tile_local, tile_slot, tile_flag, want_list):
    peers = lax.axis_size("row")
    fibres, width = forces.shape
    unknowns = tiles.shape[1]
    capacity = want_list.shape[2]
    slots = peers * capacity
    wanted = want_list[0]
    start = forces.reshape(fibres, NRHS, unknowns)
    index = jnp.concatenate([tile_local, tile_slot, tile_flag])
    asked = lax.all_to_all(wanted, "row", 0, 0, tiled=True)
    asked, index = lax.optimization_barrier((asked, index))
    asked = asked.reshape(-1)
    first_sent, start = lax.optimization_barrier((gather(asked, start), start))
    pairs, mirrored = first_pass(index, tiles, start, slots, capacity)

    def finish(mirrored, sent, again):
        got = lax.all_to_all(mirrored, "row", 0, 0, tiled=True)
        far = lax.all_to_all(sent, "row", 0, 0, tiled=True)
        own = tile_pass(False, index, pairs, far, fibres, capacity)
        return combine(asked, own, got, capacity, again)

    one, sent = finish(mirrored, first_sent, True)
    mirrored = tile_pass(True, index, pairs, one, slots, capacity)
    (two,) = finish(mirrored, sent, False)
    return (one.reshape(fibres, width), two.reshape(fibres, width))


def solution(mesh):
    in_specs = (
        P(("groups", "row"), None),
        P(("groups", "row"), None, None),
        P(("groups", "row")),
        P(("groups", "row")),
        P(("groups", "row")),
        P(("groups", "row"), None, None),
    )
    out_specs = (P(("groups", "row"), None), P(("groups", "row"), None))
    return jax.shard_map(
        per_device, mesh=mesh, in_specs=in_specs, out_specs=out_specs, check_vma=False
    )
```
